32 devices in a mesh: groups: 2 (over x), slide: 2 (over core), seq: 8 (over z, y).
Axes of the slice: x: 2, y: 2, z: 4, core: 2. Of those that a mesh axis runs over, the one named last changes fastest.
Arguments:
- held_feats: bfloat16 [4, 8, 1024, 1536], P(('groups', 'slide'), 'seq'), parts along dimension 0, may hold values from -6 to 6
- held_pos: int32 [4, 8, 1024], P(('groups', 'slide'), 'seq'), parts along dimension 0, may hold values from 0 to 4096, as said below
- tile_count: int32 [4], P(('groups', 'slide')), parts along dimension 0, may hold values from 1024 to 4096, as said below
- tile_gain: float32 [1536], replicated, may hold values from 0.25 to 1.75
- w_tile: bfloat16 [1536, 768], replicated, may hold values from -0.15625 to 0.15625
- slide_gain: float32 [768], replicated, may hold values from 0.25 to 1.75
- w_qkv: bfloat16 [768, 2304], replicated, may hold values from -1.5 to 1.5
- w_out: bfloat16 [768, 768], replicated, may hold values from -0.21875 to 0.21875
Outputs:
- slide_out: bfloat16 [4, 4096, 768], P(('groups', 'slide'), 'seq'), parts along dimension 0
The draws below stay inside these ranges and needn't reach their ends.
There are 2 independent parts, one for each index of `groups`. The reference program is written for one: setup_inputs(seed, part) draws one part's arguments, and reference() takes and returns one part's arrays. A program takes and returns all parts, laid end to end along the dimension named above; an argument that names none is the same for every part. Nothing has to cross between parts.
Inputs may be any that keep to these rules, and one draw needn't show every extreme that they name: `held_pos`: slot block d (slots d * 128 to (d + 1) * 128 - 1) of every device holds only positions from d * 512 to (d + 1) * 512 - 1, its live slots first in increasing position, the rest 4096. Each position below the slide's tile_count is held by exactly one slot, no other position by any. `tile_count`: one of the two slides of a part has all 4096 tiles.
All inputs are finite; a program needn't handle non-finite values.
Results may differ from the reference program's by a relative error of at most 0.0025.
The reference program's roundings to bfloat16 on the way count: a program that leaves them out, or rounds other values in their place, can miss the bound.
Values may be sent and summed in bfloat16 or wider, within the bound.
A program may use at most 128 MiB of HBM per device.

```python
import math
import jax
import jax.numpy as jnp
from jax import lax

TILE_W = 1536
SLIDE_WIDTH = 768
HEADS = 16
HEAD_DIM = 48
TILE_DEV = 512
SEG_LOC = 512
MIDDLE_DILATION = 8
UPPER_DILATION = 16
SLOTS = 1024
CAP = 128
SEQ_LEN = 4096
N_SEQ = 8


def layout_helper(key):
    seq_devices = SEQ_LEN // TILE_DEV
    count_key, order_key, first_key, longest_key = jax.random.split(key, 4)
    shortest = SEQ_LEN // 4
    counts = jax.random.randint(count_key, (2,), shortest, SEQ_LEN + 1)
    longest = jax.random.randint(longest_key, (), 0, 2)
    counts = jnp.where(jnp.arange(2) == longest, SEQ_LEN, counts).astype(jnp.int32)
    sources = jnp.repeat(jnp.arange(seq_devices, dtype=jnp.int32), CAP)
    first_sources = jax.random.randint(first_key, (2, seq_devices), 0, seq_devices)

    def one_block(slide_index, first_source, target_device, slide_total):
        block_key = jax.random.fold_in(order_key, slide_index * seq_devices + target_device)
        jitter = jax.random.randint(block_key, (SLOTS,), 0, 1 << 18)
        indices = jnp.arange(SLOTS, dtype=jnp.int32)
        scores = jitter * SLOTS + indices
        scores = jnp.where(sources == first_source, indices - SLOTS, scores)
        ordering = jnp.argsort(scores, stable=True)
        holder = sources[ordering[:TILE_DEV]]
        onehot = (holder[:, None] == jnp.arange(seq_devices, dtype=jnp.int32)[None, :]).astype(jnp.int32)
        ranking = jnp.sum((jnp.cumsum(onehot, axis=0) - onehot) * onehot, axis=1)
        position = target_device * TILE_DEV + jnp.arange(TILE_DEV, dtype=jnp.int32)
        entries = jnp.where(position < slide_total, position, SEQ_LEN).astype(jnp.int32)
        layout = jnp.full((seq_devices, SLOTS), SEQ_LEN, jnp.int32)
        return layout.at[holder, target_device * CAP + ranking].set(entries)
    devices = jnp.arange(seq_devices, dtype=jnp.int32)
    slide_indices = jnp.arange(2, dtype=jnp.int32)
    per_slide = jax.vmap(jax.vmap(one_block, in_axes=(None, 0, 0, None)), in_axes=(0, 0, None, 0))
    tables = per_slide(slide_indices, first_sources, devices, counts)
    return (counts, jnp.min(tables, axis=1).astype(jnp.int32))


def draw_held_pos(key, part):
    return layout_helper(key)[1]


def draw_tile_count(key, part):
    return layout_helper(key)[0]


def draw_w_qkv(key, part):
    key = jax.random.fold_in(key, 7)
    base_key = jax.random.fold_in(key, 0)
    fan_scale = SLIDE_WIDTH ** (-0.5)
    normal_part = jnp.clip(jax.random.normal(base_key, (SLIDE_WIDTH, 3 * SLIDE_WIDTH), jnp.float32), -6.0, 6.0)
    return (normal_part * fan_scale).astype(jnp.bfloat16)


def shard_levels(key, dims, shards, least, top_value):
    loudness, own = 1.0, jax.random.fold_in(key, 6)
    for axis_at, shards_of in shards:
        draws = jnp.exp(jax.random.uniform(jax.random.fold_in(own, axis_at), (shards_of,), jnp.float32, least / len(shards), top_value / len(shards)))
        loudness = loudness * jnp.repeat(draws, dims[axis_at] // shards_of).reshape([-1 if axis == axis_at else 1 for axis in range(len(dims))])
    return loudness


def centred(rng, extent, width, bound, shards=(), kind=jnp.bfloat16):
    result = width * jax.random.normal(rng, extent, jnp.float32)
    if shards:
        result = result * shard_levels(rng, extent, shards, -0.22, 0.18)
    return jnp.clip(result, -bound, bound).astype(kind)


def setup_inputs(seed: int = 0, part: int = 0) -> dict:
    seeds = jax.random.split(jax.random.key(seed), 9)
    own_keys = jax.random.split(jax.random.fold_in(seeds[8], part), 9)
    return {
        "held_feats": centred(own_keys[0], (2, N_SEQ, SLOTS, TILE_W), 1.0, 6.0, ((0, 2), (1, 8))),
        "held_pos": draw_held_pos(jax.random.fold_in(jax.random.fold_in(seeds[8], part), 71), part),
        "tile_count": draw_tile_count(jax.random.fold_in(jax.random.fold_in(seeds[8], part), 71), part),
        "tile_gain": jnp.clip(1.0 + 0.15 * jax.random.normal(seeds[3], (TILE_W,), jnp.float32), 0.25, 1.75),
        "w_tile": centred(seeds[4], (TILE_W, SLIDE_WIDTH), TILE_W ** -0.5, 0.15625),
        "slide_gain": jnp.clip(1.0 + 0.15 * jax.random.normal(seeds[5], (SLIDE_WIDTH,), jnp.float32), 0.25, 1.75),
        "w_qkv": draw_w_qkv(jax.random.fold_in(seeds[8], 71), part),
        "w_out": centred(seeds[7], (SLIDE_WIDTH, SLIDE_WIDTH), SLIDE_WIDTH ** -0.5, 0.21875),
    }


NEGATIVE = -1e+30
EPSILON = 1e-06

def layer_norm(values, norm_gain):
    values = values.astype(jnp.float32)
    center = values - lax.optimization_barrier(jnp.mean(values, axis=-1, keepdims=True))
    spread = lax.optimization_barrier(jnp.mean(center * center, axis=-1, keepdims=True))
    return center * lax.rsqrt(spread + EPSILON) * norm_gain.astype(jnp.float32)

def pick_table(stride, head_count):
    return jnp.arange(stride)[:, None] == (jnp.arange(head_count) % stride)[None, :]

def picked_rows(values, stride):
    row_total, head_count = (values.shape[0], values.shape[1])
    shaped = values.reshape((row_total // stride, stride) + values.shape[1:])
    chosen_mask = pick_table(stride, head_count).reshape((1, stride, head_count) + (1,) * (values.ndim - 2))
    return lax.optimization_barrier(jnp.sum(jnp.where(chosen_mask, shaped, jnp.zeros((), values.dtype)), axis=1)).astype(values.dtype)

def spread_rows(values, stride, filler):
    head_count = values.shape[1]
    chosen_mask = pick_table(stride, head_count).reshape((1, stride, head_count) + (1,) * (values.ndim - 2))
    widened = jnp.where(chosen_mask, values[:, None], jnp.asarray(filler, values.dtype))
    return widened.reshape((values.shape[0] * stride,) + values.shape[1:])

def dilated_scores(queries, far_keys, stride, tile_total, scaling):
    chosen = picked_rows(queries, stride)
    scores = jnp.einsum('qhd,khd->hqk', chosen.astype(jnp.float32), far_keys.astype(jnp.float32)) * scaling
    head_count = queries.shape[1]
    key_place = jnp.arange(far_keys.shape[0])[:, None] * stride + (jnp.arange(head_count) % stride)[None, :]
    allowed = jnp.transpose(key_place < tile_total)[:, None, :]
    return (jnp.where(allowed, scores, NEGATIVE), allowed)

def attend_sets(queries, key_matrix, value_matrix, distant_groups, first_row, tile_total):
    row_total, head_count, head_width = queries.shape
    scaling = 1.0 / math.sqrt(head_width)
    blocks = row_total // SEG_LOC

    def local_shape(values):
        return values.reshape(blocks, SEG_LOC, head_count, head_width)
    local = jnp.einsum('nqhd,nkhd->nhqk', local_shape(queries).astype(jnp.float32), local_shape(key_matrix).astype(jnp.float32)) * scaling
    key_valid = (first_row + jnp.arange(row_total) < tile_total).reshape(blocks, 1, 1, SEG_LOC)
    local = jnp.where(key_valid, local, NEGATIVE)
    highest = jnp.transpose(lax.optimization_barrier(jnp.max(local, axis=-1)), (0, 2, 1)).reshape(row_total, head_count)
    far_scores = []
    for stride, far_keys, far_values in distant_groups:
        scores, allowed = dilated_scores(queries, far_keys, stride, tile_total, scaling)
        far_scores.append((stride, scores, allowed, far_values))
        highest = jnp.maximum(highest, spread_rows(jnp.transpose(lax.optimization_barrier(jnp.max(scores, axis=-1))), stride, NEGATIVE))
    local_high = jnp.transpose(highest.reshape(blocks, SEG_LOC, head_count), (0, 2, 1))[..., None]
    weights = jnp.where(key_valid, jnp.exp(local - local_high), 0.0)
    denominator = jnp.transpose(lax.optimization_barrier(jnp.sum(weights, axis=-1)), (0, 2, 1)).reshape(row_total, head_count)
    summed = jnp.einsum('nhqk,nkhd->nqhd', weights.astype(jnp.bfloat16).astype(jnp.float32), local_shape(value_matrix).astype(jnp.float32))
    summed = summed.reshape(row_total, head_count, head_width)
    for stride, scores, allowed, far_values in far_scores:
        chosen_high = jnp.transpose(picked_rows(highest, stride))[:, :, None]
        weights = jnp.where(allowed, jnp.exp(scores - chosen_high), 0.0)
        denominator = denominator + spread_rows(jnp.transpose(lax.optimization_barrier(jnp.sum(weights, axis=-1))), stride, 0.0)
        portion = jnp.einsum('hqk,khd->qhd', weights.astype(jnp.bfloat16).astype(jnp.float32), far_values.astype(jnp.float32))
        summed = summed + spread_rows(portion, stride, 0.0)
    row_valid = first_row + jnp.arange(row_total) < tile_total
    divisor = jnp.where(row_valid[:, None], denominator, 1.0)
    attention = jnp.where(row_valid[:, None, None], summed / divisor[:, :, None], 0.0)
    return (attention.astype(jnp.bfloat16).reshape(row_total, head_count * head_width), row_valid)

def reference(held_feats, held_pos, tile_count, tile_gain, w_tile, slide_gain, w_qkv, w_out):
    normed_tiles = layer_norm(held_feats, tile_gain).astype(jnp.bfloat16)
    embedded = jnp.dot(normed_tiles.reshape(-1, TILE_W), w_tile, preferred_element_type=jnp.float32).astype(jnp.bfloat16)
    embedded = embedded.reshape(2, -1, SLIDE_WIDTH)
    targets = held_pos.reshape(2, -1)

    def place(target, row_values):
        return jnp.zeros((SEQ_LEN + 1, SLIDE_WIDTH), jnp.bfloat16).at[target].set(row_values)[:SEQ_LEN]
    placed = jax.vmap(place)(targets, embedded)

    def encode(inputs):
        tokens, tile_total = inputs
        normed = layer_norm(tokens, slide_gain).astype(jnp.bfloat16)
        projected = jnp.dot(normed, w_qkv, preferred_element_type=jnp.float32).astype(jnp.bfloat16)
        queries = projected[:, :SLIDE_WIDTH].reshape(SEQ_LEN, HEADS, HEAD_DIM)
        key_matrix = projected[:, SLIDE_WIDTH:2 * SLIDE_WIDTH].reshape(SEQ_LEN, HEADS, HEAD_DIM)
        value_matrix = projected[:, 2 * SLIDE_WIDTH:].reshape(SEQ_LEN, HEADS, HEAD_DIM)
        distant_groups = [(MIDDLE_DILATION, picked_rows(key_matrix, MIDDLE_DILATION), picked_rows(value_matrix, MIDDLE_DILATION)), (UPPER_DILATION, picked_rows(key_matrix, UPPER_DILATION), picked_rows(value_matrix, UPPER_DILATION))]
        attention, row_valid = attend_sets(queries, key_matrix, value_matrix, distant_groups, 0, tile_total)
        updated = tokens.astype(jnp.float32) + jnp.dot(attention, w_out, preferred_element_type=jnp.float32)
        return jnp.where(row_valid[:, None], updated, 0.0).astype(jnp.bfloat16)
    return lax.map(encode, (placed, tile_count))
```

```python
import functools
import math

import jax
import jax.numpy as jnp
from jax import lax
from jax.experimental import pallas as pl
from jax.experimental.pallas import tpu as pltpu
from jax.sharding import PartitionSpec as P

SLIDE_WIDTH = 768
HEADS = 16
HEAD_DIM = 48
TILE_DEV = 512
STRIDE = 8
ROWS = TILE_DEV // STRIDE
TILES = 8
LANES = 128
NEGATIVE = -1e30
EPSILON = 1e-06
C = math.log2(math.e) / math.sqrt(HEAD_DIM)
F32 = jnp.float32
BF16 = jnp.bfloat16


def dot(a, b):
    return jnp.dot(a, b, preferred_element_type=F32)


def dot_t(a, b):
    return lax.dot_general(a, b, (((1,), (1,)), ((), ())), preferred_element_type=F32)


def normalise(values, gain):
    center = values - jnp.mean(values, axis=-1, keepdims=True)
    spread = jnp.mean(center * center, axis=-1, keepdims=True)
    return (center * lax.rsqrt(spread + EPSILON) * gain).astype(BF16)


def flip(a, b, size):
    total, bit = 0, 1
    while bit < size:
        total = total + bit * (((a // bit) % 2 + (b // bit) % 2) % 2)
        bit *= 2
    return total


def iota(shape, axis):
    return lax.broadcasted_iota(jnp.int32, shape, axis)


def soft_parts(q, k, v, half_mask, weigh):
    raw = dot_t(q, jnp.where(half_mask, k, jnp.zeros_like(k)))
    top = jnp.max(raw, axis=1, keepdims=True)
    weights = jnp.exp2((raw - top) * C)
    if weigh is not None:
        weights = weights * weigh
    return dot(weights.astype(BF16), v), jnp.sum(weights, axis=1, keepdims=True), top


def kernel(
    n, feats, pos, count, tile_gain, w_tile, slide_gain, w_qkv, w_out, out,
    x_v, wt_v, wq_v, wo_v, wq_pad, wo_pad, emb, arrived, spots, tokens, proj, picks, mids,
    ret_out, ret_in, attn, local_pick,
    x_sem, w_sem, es, er, ps, pr, ms, mr, rs, rr,
):
    me = lax.axis_index("seq")
    groups = n // TILES
    group, mine = me // TILES, me % TILES
    first = me * TILE_DEV
    total = count[0]

    def x_copy(d):
        return pltpu.make_async_copy(feats.at[d], x_v.at[d], x_sem.at[d])

    w_copies = [
        pltpu.make_async_copy(w_tile, wt_v, w_sem.at[0]),
        pltpu.make_async_copy(w_qkv, wq_v, w_sem.at[1]),
        pltpu.make_async_copy(w_out, wo_v, w_sem.at[2]),
    ]
    x_copy(flip(me, n - 1, n)).start()
    w_copies[0].start()

    @pl.loop(1, n)
    def _(i):
        x_copy(flip(me, n - 1 - i, n)).start()

    w_copies[1].start()
    w_copies[2].start()

    barrier = pltpu.get_barrier_semaphore()

    @pl.loop(1, n)
    def _(i):
        pl.semaphore_signal(
            barrier, inc=1, device_id={"seq": (me + i) % n}, device_id_type=pl.DeviceIdType.MESH
        )

    pl.semaphore_wait(barrier, n - 1)

    def remote(src, dst, send, recv, device):
        return pltpu.make_async_remote_copy(
            src_ref=src, dst_ref=dst, send_sem=send, recv_sem=recv,
            device_id={"seq": device}, device_id_type=pl.DeviceIdType.MESH,
        )

    def emb_copy(d, slot):
        return remote(emb.at[d], arrived.at[slot], es.at[d], er.at[slot], d)

    def pos_copy(d, slot):
        return remote(pos.at[d], spots.at[slot], ps.at[d], pr.at[slot], d)

    @pl.loop(0, n - 1)
    def _(i):
        d = flip(me, n - 1 - i, n)
        pos_copy(d, me).start()

    w_copies[0].wait()

    def embed(d):
        x_copy(d).wait()
        normed = normalise(x_v[d].astype(F32), tile_gain[...])
        return dot(normed, wt_v[...]).astype(BF16)

    @pl.loop(0, n - 1)
    def _(i):
        d = flip(me, n - 1 - i, n)
        emb[d] = embed(d)
        emb_copy(d, me).start()

    arrived[me] = embed(me)
    spots[me] = pos[me]

    w_copies[1].wait()
    w_copies[2].wait()

    @pl.loop(0, TILES)
    def _(r):
        def wanted(t):
            half = t // 64
            feature = t % 64
            column = (r + TILES * half) * HEAD_DIM + feature
            return jnp.where(feature < HEAD_DIM, column, -1)

        widen = jnp.where(
            iota((SLIDE_WIDTH, LANES), 0) == wanted(iota((SLIDE_WIDTH, LANES), 1)), 1.0, 0.0
        ).astype(BF16)
        for part in range(3):
            wq_pad[r, :, part * LANES : (part + 1) * LANES] = dot(
                wq_v[:, part * SLIDE_WIDTH : (part + 1) * SLIDE_WIDTH], widen
            ).astype(BF16)
        widen_t = jnp.where(
            iota((LANES, SLIDE_WIDTH), 1) == wanted(iota((LANES, SLIDE_WIDTH), 0)), 1.0, 0.0
        ).astype(BF16)
        wo_pad[r] = dot(widen_t, wo_v[...]).astype(BF16)

    cap = spots.shape[2]

    def place(s):
        hot = jnp.where(iota((TILE_DEV, cap), 0) + first == spots[s], 1.0, 0.0).astype(BF16)
        return dot(hot, arrived[s])

    tokens[...] = place(me)

    @pl.loop(0, n - 1)
    def _(i):
        s = flip(me, n - 1 - i, n)
        pos_copy(s, s).wait_recv()
        emb_copy(s, s).wait_recv()
        tokens[...] += place(s)

    normed = normalise(tokens[...], slide_gain[...])

    def half_lane(shape):
        return iota(shape, 1) % 64

    def gather_rows(r):
        return jnp.where(
            iota((ROWS, TILE_DEV), 1) == STRIDE * iota((ROWS, TILE_DEV), 0) + r, 1.0, 0.0
        ).astype(BF16)

    def mid_copy(r, g, slot):
        d = g * TILES + r
        return remote(picks.at[r], mids.at[slot], ms.at[d], mr.at[slot], d)

    lane3 = iota((TILE_DEV, 3 * LANES), 1)
    is_bias = lane3 % 64 == HEAD_DIM
    valid3 = iota((TILE_DEV, 3 * LANES), 0) + first < total
    bias = jnp.where(
        lane3 < LANES, 1.0, jnp.where((lane3 < 2 * LANES) & (~valid3), NEGATIVE, 0.0)
    )
    extra = jnp.where(is_bias, bias, 0.0)

    def project(r):
        made = (dot(normed, wq_pad[r]) + extra).astype(BF16)
        proj[r] = made
        picked = dot(gather_rows(r), made).astype(BF16)
        return picked

    @pl.loop(0, TILES - 1)
    def _(i):
        r = flip(mine, TILES - 1 - i, TILES)
        picks[r] = project(r)
        for g in range(groups):
            mid_copy(r, g, me).start()

    own_pick = project(mine)
    mids[me] = own_pick
    if groups > 1:
        picks[mine] = own_pick
        for step in range(1, groups):
            mid_copy(mine, (group + step) % groups, me).start()

    lane = iota((TILE_DEV, LANES), 1)
    low = lane < 64

    def half_masks(shape):
        side = iota(shape, 1) < 64
        return side, ~side

    def pack(parts):
        (n0, d0, t0), (n1, d1, t1) = parts
        mixed = jnp.where(low, n0, n1)
        return jnp.where(
            lane == 48, d0, jnp.where(lane == 49, t0,
            jnp.where(lane == 112, d1, jnp.where(lane == 113, t1, mixed))))

    def local_tile(r):
        q = proj[r, :, :LANES]
        k = proj[r, :, LANES : 2 * LANES]
        v = proj[r, :, 2 * LANES :]
        parts = [soft_parts(q, k, v, mask, None) for mask in half_masks(k.shape)]
        (n0, d0, _), (n1, d1, _) = parts
        packed = pack(parts)
        row = iota((TILE_DEV, LANES), 0)
        chosen = row % STRIDE == r
        share = jnp.where(low, n0 / d0, n1 / d1)
        keep = (~chosen) & (row + first < total)
        attn[r] = jnp.where(keep, share, 0.0).astype(BF16)
        local_pick[r] = jnp.sum(
            jnp.where(chosen, packed, 0.0).reshape(ROWS, STRIDE, LANES), axis=1
        )

    before = 5

    @pl.loop(0, before)
    def _(r):
        local_tile(r)

    def ret_copy(t, slot):
        return remote(ret_out.at[t], ret_in.at[slot], rs.at[t], rr.at[slot], group * TILES + t)

    @pl.loop(1, n)
    def _(i):
        s = flip(me, n - i, n)
        remote(mids.at[s], mids.at[s], ms.at[s], mr.at[s], s).wait_recv()

    far_q = mids[pl.ds(group * TILES, TILES), :, :LANES].reshape(TILES * ROWS, LANES)
    far_k = mids[:, :, LANES : 2 * LANES].reshape(n * ROWS, LANES)
    far_v = mids[:, :, 2 * LANES :].reshape(n * ROWS, LANES)
    far_parts = []
    shape = (TILES * ROWS, n * ROWS)
    for half, mask in enumerate(half_masks(far_k.shape)):
        both = (iota(shape, 0) % 2 == half) & (iota(shape, 1) % 2 == half)
        far_parts.append(soft_parts(far_q, far_k, far_v, mask, jnp.where(both, 2.0, 1.0)))
    ret_out[...] = pack(far_parts).reshape(TILES, ROWS, LANES)

    @pl.loop(0, TILES - 1)
    def _(i):
        ret_copy(flip(mine, TILES - 1 - i, TILES), mine).start()

    ret_in[mine] = ret_out[mine]

    @pl.loop(before, TILES)
    def _(r):
        local_tile(r)

    @pl.loop(0, TILES - 1)
    def _(i):
        t = flip(mine, TILES - 1 - i, TILES)
        ret_copy(t, t).wait_recv()

    acc = tokens[...]
    small = iota((ROWS, LANES), 1)
    for r in range(TILES):
        here, there = local_pick[r], ret_in[r]

        def joined(at):
            top = jnp.maximum(here[:, at + 1 : at + 2], there[:, at + 1 : at + 2])
            a = jnp.exp2((here[:, at + 1 : at + 2] - top) * C)
            b = jnp.exp2((there[:, at + 1 : at + 2] - top) * C)
            return (a * here + b * there) / (
                a * here[:, at : at + 1] + b * there[:, at : at + 1]
            )

        share = jnp.where(small < 64, joined(48), joined(112))
        share = jnp.where(small % 64 < HEAD_DIM, share, 0.0)
        valid = iota((ROWS, LANES), 0) * STRIDE + r + first < total
        share = jnp.where(valid, share, 0.0).astype(BF16)
        back = jnp.where(
            iota((TILE_DEV, ROWS), 0) == STRIDE * iota((TILE_DEV, ROWS), 1) + r, 1.0, 0.0
        ).astype(BF16)
        whole = (attn[r].astype(F32) + dot(back, share)).astype(BF16)
        acc = acc + dot(whole, wo_pad[r])
    out[...] = jnp.where(iota((TILE_DEV, 1), 0) + first < total, acc, 0.0).astype(BF16)

    @pl.loop(0, n - 1)
    def _(i):
        d = flip(me, n - 1 - i, n)
        pos_copy(d, me).wait_send()
        emb_copy(d, me).wait_send()
        mid_copy(d % TILES, d // TILES, me).wait_send()

    @pl.loop(0, TILES - 1)
    def _(i):
        ret_copy(flip(mine, TILES - 1 - i, TILES), mine).wait_send()


def shards(n, held_feats, held_pos, tile_count, tile_gain, w_tile, slide_gain, w_qkv, w_out):
    slots, width = held_feats.shape[2:]
    cap = slots // n
    vmem = pl.BlockSpec(memory_space=pltpu.VMEM)
    hbm = pl.BlockSpec(memory_space=pl.ANY)
    smem = pl.BlockSpec(memory_space=pltpu.SMEM)
    dma = pltpu.SemaphoreType.DMA
    result = pl.pallas_call(
        functools.partial(kernel, n),
        out_shape=jax.ShapeDtypeStruct((TILE_DEV, SLIDE_WIDTH), BF16),
        in_specs=[hbm, vmem, smem, vmem, hbm, vmem, hbm, hbm],
        out_specs=vmem,
        scratch_shapes=[
            pltpu.VMEM((n, cap, width), BF16),
            pltpu.VMEM(w_tile.shape, BF16),
            pltpu.VMEM(w_qkv.shape, BF16),
            pltpu.VMEM(w_out.shape, BF16),
            pltpu.VMEM((TILES, SLIDE_WIDTH, 3 * LANES), BF16),
            pltpu.VMEM((TILES, LANES, SLIDE_WIDTH), BF16),
            pltpu.VMEM((n, cap, SLIDE_WIDTH), BF16),
            pltpu.VMEM((n, cap, SLIDE_WIDTH), BF16),
            pltpu.VMEM((n, 1, cap), jnp.int32),
            pltpu.VMEM((TILE_DEV, SLIDE_WIDTH), F32),
            pltpu.VMEM((TILES, TILE_DEV, 3 * LANES), BF16),
            pltpu.VMEM((TILES, ROWS, 3 * LANES), BF16),
            pltpu.VMEM((n, ROWS, 3 * LANES), BF16),
            pltpu.VMEM((TILES, ROWS, LANES), F32),
            pltpu.VMEM((TILES, ROWS, LANES), F32),
            pltpu.VMEM((TILES, TILE_DEV, LANES), BF16),
            pltpu.VMEM((TILES, ROWS, LANES), F32),
            dma((n,)), dma((3,)),
            dma((n,)), dma((n,)), dma((n,)), dma((n,)),
            dma((n,)), dma((n,)), dma((TILES,)), dma((TILES,)),
        ],
        compiler_params=pltpu.CompilerParams(
            collective_id=0, has_side_effects=True, vmem_limit_bytes=58 * 1024 * 1024
        ),
        name="slide_layer",
    )(
        held_feats.reshape(n, cap, width),
        held_pos.reshape(n, 1, cap),
        tile_count,
        tile_gain.reshape(1, width),
        w_tile,
        slide_gain.reshape(1, SLIDE_WIDTH),
        w_qkv,
        w_out,
    )
    return result.reshape(1, TILE_DEV, SLIDE_WIDTH)


def solution(mesh):
    n = mesh.shape["seq"]
    return jax.shard_map(
        functools.partial(shards, n),
        mesh=mesh,
        in_specs=(
            P(("groups", "slide"), "seq", None, None),
            P(("groups", "slide"), "seq", None),
            P(("groups", "slide")),
            P(), P(), P(), P(), P(),
        ),
        out_specs=P(("groups", "slide"), "seq", None),
        check_vma=False,
    )
```

```python
import functools
import math

import jax
import jax.numpy as jnp
from jax import lax
from jax.experimental import pallas as pl
from jax.experimental.pallas import tpu as pltpu
from jax.sharding import PartitionSpec as P

SLIDE_WIDTH = 768
HEADS = 16
HEAD_DIM = 48
TILE_DEV = 512
STRIDE = 8
ROWS = TILE_DEV // STRIDE
TILES = 8
LANES = 128
NEGATIVE = -1e30
EPSILON = 1e-06
C = math.log2(math.e) / math.sqrt(HEAD_DIM)
F32 = jnp.float32
BF16 = jnp.bfloat16


def dot(a, b):
    return jnp.dot(a, b, preferred_element_type=F32)


def dot_t(a, b):
    return lax.dot_general(a, b, (((1,), (1,)), ((), ())), preferred_element_type=F32)


def normalise(values, gain):
    center = values - jnp.mean(values, axis=-1, keepdims=True)
    spread = jnp.mean(center * center, axis=-1, keepdims=True)
    return (center * lax.rsqrt(spread + EPSILON) * gain).astype(BF16)


def flip(a, b, size):
    total, bit = 0, 1
    while bit < size:
        total = total + bit * (((a // bit) % 2 + (b // bit) % 2) % 2)
        bit *= 2
    return total


def iota(shape, axis):
    return lax.broadcasted_iota(jnp.int32, shape, axis)


def soft_parts(q, k, v, half_mask, weigh):
    raw = dot_t(q, jnp.where(half_mask, k, jnp.zeros_like(k)))
    top = jnp.max(raw, axis=1, keepdims=True)
    weights = jnp.exp2((raw - top) * C)
    if weigh is not None:
        weights = weights * weigh
    return dot(weights.astype(BF16), v), jnp.sum(weights, axis=1, keepdims=True), top


def kernel(
    n, feats, pos, count, tile_gain, w_tile, slide_gain, w_qkv, w_out, out,
    x_v, wt_v, wq_v, wo_v, wq_pad, wo_pad, emb, arrived, spots, tokens, flat, sorted_rows, picks, mids,
    ret_out, ret_in, local_pick,
    x_sem, w_sem, es, er, ps, pr, ms, mr, rs, rr,
):
    me = lax.axis_index("seq")
    groups = n // TILES
    group, mine = me // TILES, me % TILES
    first = me * TILE_DEV
    total = count[0]

    def x_copy(d):
        return pltpu.make_async_copy(feats.at[d], x_v.at[d], x_sem.at[d])

    w_copies = [
        pltpu.make_async_copy(w_tile, wt_v, w_sem.at[0]),
        pltpu.make_async_copy(w_qkv, wq_v, w_sem.at[1]),
        pltpu.make_async_copy(w_out, wo_v, w_sem.at[2]),
    ]
    x_copy(flip(me, n - 1, n)).start()
    w_copies[0].start()

    @pl.loop(1, n)
    def _(i):
        x_copy(flip(me, n - 1 - i, n)).start()

    w_copies[1].start()
    w_copies[2].start()

    barrier = pltpu.get_barrier_semaphore()

    @pl.loop(1, n)
    def _(i):
        pl.semaphore_signal(
            barrier, inc=1, device_id={"seq": (me + i) % n}, device_id_type=pl.DeviceIdType.MESH
        )

    pl.semaphore_wait(barrier, n - 1)

    def remote(src, dst, send, recv, device):
        return pltpu.make_async_remote_copy(
            src_ref=src, dst_ref=dst, send_sem=send, recv_sem=recv,
            device_id={"seq": device}, device_id_type=pl.DeviceIdType.MESH,
        )

    def emb_copy(d, slot):
        return remote(emb.at[d], arrived.at[slot], es.at[d], er.at[slot], d)

    def pos_copy(d, slot):
        return remote(pos.at[d], spots.at[slot], ps.at[d], pr.at[slot], d)

    @pl.loop(0, n - 1)
    def _(i):
        d = flip(me, n - 1 - i, n)
        pos_copy(d, me).start()

    w_copies[0].wait()

    def embed(d):
        x_copy(d).wait()
        normed = normalise(x_v[d].astype(F32), tile_gain[...][None, :])
        return dot(normed, wt_v[...]).astype(BF16)

    @pl.loop(0, n - 1)
    def _(i):
        d = flip(me, n - 1 - i, n)
        emb[d] = embed(d)
        emb_copy(d, me).start()

    arrived[me] = embed(me)
    spots[me] = pos[me]

    w_copies[1].wait()
    w_copies[2].wait()

    @pl.loop(0, TILES)
    def _(r):
        def wanted(t):
            half = t // 64
            feature = t % 64
            column = (r + TILES * half) * HEAD_DIM + feature
            return jnp.where(feature < HEAD_DIM, column, -1)

        widen = jnp.where(
            iota((SLIDE_WIDTH, LANES), 0) == wanted(iota((SLIDE_WIDTH, LANES), 1)), 1.0, 0.0
        ).astype(BF16)
        for part in range(3):
            wq_pad[r, :, part * LANES : (part + 1) * LANES] = dot(
                wq_v[:, part * SLIDE_WIDTH : (part + 1) * SLIDE_WIDTH], widen
            ).astype(BF16)
        widen_t = jnp.where(
            iota((LANES, SLIDE_WIDTH), 1) == wanted(iota((LANES, SLIDE_WIDTH), 0)), 1.0, 0.0
        ).astype(BF16)
        wo_pad[r] = dot(widen_t, wo_v[...]).astype(BF16)

    cap = spots.shape[2]

    def place(s):
        hot = jnp.where(iota((TILE_DEV, cap), 0) + first == spots[s], 1.0, 0.0).astype(BF16)
        return dot(hot, arrived[s])

    tokens[...] = place(me)

    def take(s):
        pos_copy(s, s).wait_recv()
        emb_copy(s, s).wait_recv()
        tokens[...] += place(s)

    @pl.loop(1, n // 2)
    def _(i):
        take(flip(me, i, n))

    @pl.loop(0, n // 2)
    def _(i):
        take(flip(me, n - 1 - i, n))

    normed = normalise(tokens[...], slide_gain[...][None, :])

    row_of = iota((TILE_DEV, TILE_DEV), 0)
    regroup = jnp.where(
        iota((TILE_DEV, TILE_DEV), 1) == STRIDE * (row_of % ROWS) + row_of // ROWS, 1.0, 0.0
    ).astype(BF16)
    sorted_rows[...] = dot(regroup, normed).astype(BF16).reshape(TILES, ROWS, SLIDE_WIDTH)
    flat[...] = normed

    def mid_copy(r, g, slot):
        d = g * TILES + r
        return remote(picks.at[r], mids.at[slot], ms.at[d], mr.at[slot], d)

    def bias(rows, step, start):
        lane3 = iota((rows, 3 * LANES), 1)
        valid = iota((rows, 3 * LANES), 0) * step + start + first < total
        value = jnp.where(
            lane3 < LANES, 1.0, jnp.where((lane3 < 2 * LANES) & (~valid), NEGATIVE, 0.0)
        )
        return jnp.where(lane3 % 64 == HEAD_DIM, value, 0.0)

    def project(r):
        return (dot(sorted_rows[r], wq_pad[r]) + bias(ROWS, STRIDE, r)).astype(BF16)

    @pl.loop(0, TILES - 1)
    def _(i):
        r = flip(mine, TILES - 1 - i, TILES)
        picks[r] = project(r)
        for g in range(groups):
            mid_copy(r, g, me).start()

    own_pick = project(mine)
    mids[me] = own_pick
    if groups > 1:
        picks[mine] = own_pick
        for step in range(1, groups):
            mid_copy(mine, (group + step) % groups, me).start()

    lane = iota((TILE_DEV, LANES), 1)
    low = lane < 64

    def half_masks(shape):
        side = iota(shape, 1) < 64
        return side, ~side

    def pack(parts):
        (n0, d0, t0), (n1, d1, t1) = parts
        mixed = jnp.where(low, n0, n1)
        return jnp.where(
            lane == 48, d0, jnp.where(lane == 49, t0,
            jnp.where(lane == 112, d1, jnp.where(lane == 113, t1, mixed))))

    def local_tile(r):
        made = (dot(flat[...], wq_pad[r]) + bias(TILE_DEV, 1, 0)).astype(BF16)
        q = made[:, :LANES]
        k = made[:, LANES : 2 * LANES]
        v = made[:, 2 * LANES :]
        parts = [soft_parts(q, k, v, mask, None) for mask in half_masks(k.shape)]
        (n0, d0, _), (n1, d1, _) = parts
        packed = pack(parts)
        row = iota((TILE_DEV, LANES), 0)
        chosen = row % STRIDE == r
        share = jnp.where(low, n0 / d0, n1 / d1)
        keep = (~chosen) & (row + first < total)
        near = jnp.where(keep, share, 0.0).astype(BF16)
        tokens[...] += dot(near, wo_pad[r])
        local_pick[r] = jnp.sum(
            jnp.where(chosen, packed, 0.0).reshape(ROWS, STRIDE, LANES), axis=1
        )

    before = 5

    @pl.loop(0, before)
    def _(r):
        local_tile(r)

    def ret_copy(t, slot):
        return remote(ret_out.at[t], ret_in.at[slot], rs.at[t], rr.at[slot], group * TILES + t)

    @pl.loop(1, n)
    def _(i):
        s = flip(me, n - i, n)
        remote(mids.at[s], mids.at[s], ms.at[s], mr.at[s], s).wait_recv()

    far_q = mids[pl.ds(group * TILES, TILES), :, :LANES].reshape(TILES * ROWS, LANES)
    far_k = mids[:, :, LANES : 2 * LANES].reshape(n * ROWS, LANES)
    far_v = mids[:, :, 2 * LANES :].reshape(n * ROWS, LANES)
    far_parts = []
    shape = (TILES * ROWS, n * ROWS)
    for half, mask in enumerate(half_masks(far_k.shape)):
        both = (iota(shape, 0) % 2 == half) & (iota(shape, 1) % 2 == half)
        far_parts.append(soft_parts(far_q, far_k, far_v, mask, jnp.where(both, 2.0, 1.0)))
    ret_out[...] = pack(far_parts).reshape(TILES, ROWS, LANES)

    @pl.loop(0, TILES - 1)
    def _(i):
        ret_copy(flip(mine, TILES - 1 - i, TILES), mine).start()

    ret_in[mine] = ret_out[mine]

    @pl.loop(before, TILES)
    def _(r):
        local_tile(r)

    @pl.loop(0, TILES - 1)
    def _(i):
        t = flip(mine, TILES - 1 - i, TILES)
        ret_copy(t, t).wait_recv()

    joint = []
    small = iota((ROWS, LANES), 1)
    for r in range(TILES):
        here, there = local_pick[r], ret_in[r]

        def joined(at):
            top = jnp.maximum(here[:, at + 1 : at + 2], there[:, at + 1 : at + 2])
            a = jnp.exp2((here[:, at + 1 : at + 2] - top) * C)
            b = jnp.exp2((there[:, at + 1 : at + 2] - top) * C)
            return (a * here + b * there) / (
                a * here[:, at : at + 1] + b * there[:, at : at + 1]
            )

        share = jnp.where(small < 64, joined(48), joined(112))
        share = jnp.where(small % 64 < HEAD_DIM, share, 0.0)
        valid = iota((ROWS, LANES), 0) * STRIDE + r + first < total
        share = jnp.where(valid, share, 0.0).astype(BF16)
        joint.append(dot(share, wo_pad[r])[:, None, :])
    added = jnp.concatenate(joint, axis=1).reshape(TILE_DEV, SLIDE_WIDTH)
    acc = tokens[...] + added
    out[...] = jnp.where(iota((TILE_DEV, 1), 0) + first < total, acc, 0.0).astype(BF16)

    @pl.loop(0, n - 1)
    def _(i):
        d = flip(me, n - 1 - i, n)
        pos_copy(d, me).wait_send()
        emb_copy(d, me).wait_send()
        mid_copy(d % TILES, d // TILES, me).wait_send()

    @pl.loop(0, TILES - 1)
    def _(i):
        ret_copy(flip(mine, TILES - 1 - i, TILES), mine).wait_send()


def shards(n, held_feats, held_pos, tile_count, tile_gain, w_tile, slide_gain, w_qkv, w_out):
    slots, width = held_feats.shape[2:]
    cap = slots // n
    vmem = pl.BlockSpec(memory_space=pltpu.VMEM)
    hbm = pl.BlockSpec(memory_space=pl.ANY)
    smem = pl.BlockSpec(memory_space=pltpu.SMEM)
    dma = pltpu.SemaphoreType.DMA
    result = pl.pallas_call(
        functools.partial(kernel, n),
        out_shape=jax.ShapeDtypeStruct((TILE_DEV, SLIDE_WIDTH), BF16),
        in_specs=[hbm, vmem, smem, vmem, hbm, vmem, hbm, hbm],
        out_specs=vmem,
        scratch_shapes=[
            pltpu.VMEM((n, cap, width), BF16),
            pltpu.VMEM(w_tile.shape, BF16),
            pltpu.VMEM(w_qkv.shape, BF16),
            pltpu.VMEM(w_out.shape, BF16),
            pltpu.VMEM((TILES, SLIDE_WIDTH, 3 * LANES), BF16),
            pltpu.VMEM((TILES, LANES, SLIDE_WIDTH), BF16),
            pltpu.VMEM((n, cap, SLIDE_WIDTH), BF16),
            pltpu.VMEM((n, cap, SLIDE_WIDTH), BF16),
            pltpu.VMEM((n, 1, cap), jnp.int32),
            pltpu.VMEM((TILE_DEV, SLIDE_WIDTH), F32),
            pltpu.VMEM((TILE_DEV, SLIDE_WIDTH), BF16),
            pltpu.VMEM((TILES, ROWS, SLIDE_WIDTH), BF16),
            pltpu.VMEM((TILES, ROWS, 3 * LANES), BF16),
            pltpu.VMEM((n, ROWS, 3 * LANES), BF16),
            pltpu.VMEM((TILES, ROWS, LANES), F32),
            pltpu.VMEM((TILES, ROWS, LANES), F32),
            pltpu.VMEM((TILES, ROWS, LANES), F32),
            dma((n,)), dma((3,)),
            dma((n,)), dma((n,)), dma((n,)), dma((n,)),
            dma((n,)), dma((n,)), dma((TILES,)), dma((TILES,)),
        ],
        compiler_params=pltpu.CompilerParams(
            collective_id=0, has_side_effects=True, vmem_limit_bytes=58 * 1024 * 1024
        ),
        name="slide_layer",
    )(
        held_feats.reshape(n, cap, width),
        held_pos.reshape(n, 1, cap),
        tile_count,
        tile_gain,
        w_tile,
        slide_gain,
        w_qkv,
        w_out,
    )
    return result.reshape(1, TILE_DEV, SLIDE_WIDTH)


def solution(mesh):
    n = mesh.shape["seq"]
    return jax.shard_map(
        functools.partial(shards, n),
        mesh=mesh,
        in_specs=(
            P(("groups", "slide"), "seq", None, None),
            P(("groups", "slide"), "seq", None),
            P(("groups", "slide")),
            P(), P(), P(), P(), P(),
        ),
        out_specs=P(("groups", "slide"), "seq", None),
        check_vma=False,
    )
```

```python
import functools
import math

import jax
import jax.numpy as jnp
from jax import lax
from jax.experimental import pallas as pl
from jax.experimental.pallas import tpu as pltpu
from jax.sharding import PartitionSpec as P

SLIDE_WIDTH = 768
HEADS = 16
HEAD_DIM = 48
TILE_DEV = 512
STRIDE = 8
ROWS = TILE_DEV // STRIDE
TILES = 8
LANES = 128
NEGATIVE = -1e30
EPSILON = 1e-06
C = math.log2(math.e) / math.sqrt(HEAD_DIM)
F32 = jnp.float32
BF16 = jnp.bfloat16


def dot(a, b):
    return jnp.dot(a, b, preferred_element_type=F32)


def dot_t(a, b):
    return lax.dot_general(a, b, (((1,), (1,)), ((), ())), preferred_element_type=F32)


def normalise(values, gain):
    center = values - jnp.mean(values, axis=-1, keepdims=True)
    spread = jnp.mean(center * center, axis=-1, keepdims=True)
    return (center * lax.rsqrt(spread + EPSILON) * gain).astype(BF16)


def flip(a, b, size):
    total, bit = 0, 1
    while bit < size:
        total = total + bit * (((a // bit) % 2 + (b // bit) % 2) % 2)
        bit *= 2
    return total


def iota(shape, axis):
    return lax.broadcasted_iota(jnp.int32, shape, axis)


def soft_parts(q, k, v, half_mask, weigh):
    raw = dot_t(q, jnp.where(half_mask, k, jnp.zeros_like(k)))
    top = jnp.max(raw, axis=1, keepdims=True)
    weights = jnp.exp2((raw - top) * C)
    if weigh is not None:
        weights = weights * weigh
    return dot(weights.astype(BF16), v), jnp.sum(weights, axis=1, keepdims=True), top


def kernel(
    n, feats, pos, count, tile_gain, w_tile, slide_gain, w_qkv, w_out, out,
    x_v, wt_v, wq_v, wo_v, wq_pad, wo_pad, emb, arrived, spots, tokens, flat, sorted_rows, picks, mids,
    ret_out, ret_in, attn, local_pick,
    x_sem, w_sem, es, er, ps, pr, ms, mr, rs, rr,
):
    me = lax.axis_index("seq")
    groups = n // TILES
    group, mine = me // TILES, me % TILES
    first = me * TILE_DEV
    total = count[0]

    def x_copy(d):
        return pltpu.make_async_copy(feats.at[d], x_v.at[d], x_sem.at[d])

    w_copies = [
        pltpu.make_async_copy(w_tile, wt_v, w_sem.at[0]),
        pltpu.make_async_copy(w_qkv, wq_v, w_sem.at[1]),
        pltpu.make_async_copy(w_out, wo_v, w_sem.at[2]),
    ]
    x_copy(flip(me, n - 1, n)).start()
    w_copies[0].start()

    @pl.loop(1, n)
    def _(i):
        x_copy(flip(me, n - 1 - i, n)).start()

    w_copies[1].start()
    w_copies[2].start()

    barrier = pltpu.get_barrier_semaphore()

    @pl.loop(1, n)
    def _(i):
        pl.semaphore_signal(
            barrier, inc=1, device_id={"seq": (me + i) % n}, device_id_type=pl.DeviceIdType.MESH
        )

    pl.semaphore_wait(barrier, n - 1)

    def remote(src, dst, send, recv, device):
        return pltpu.make_async_remote_copy(
            src_ref=src, dst_ref=dst, send_sem=send, recv_sem=recv,
            device_id={"seq": device}, device_id_type=pl.DeviceIdType.MESH,
        )

    def emb_copy(d, slot):
        return remote(emb.at[d], arrived.at[slot], es.at[d], er.at[slot], d)

    def pos_copy(d, slot):
        return remote(pos.at[d], spots.at[slot], ps.at[d], pr.at[slot], d)

    @pl.loop(0, n - 1)
    def _(i):
        d = flip(me, n - 1 - i, n)
        pos_copy(d, me).start()

    w_copies[0].wait()

    def embed(d):
        x_copy(d).wait()
        normed = normalise(x_v[d].astype(F32), tile_gain[...][None, :])
        return dot(normed, wt_v[...]).astype(BF16)

    @pl.loop(0, n - 1)
    def _(i):
        d = flip(me, n - 1 - i, n)
        emb[d] = embed(d)
        emb_copy(d, me).start()

    arrived[me] = embed(me)
    spots[me] = pos[me]

    w_copies[1].wait()
    w_copies[2].wait()

    @pl.loop(0, TILES)
    def _(r):
        def wanted(t):
            half = t // 64
            feature = t % 64
            column = (r + TILES * half) * HEAD_DIM + feature
            return jnp.where(feature < HEAD_DIM, column, -1)

        widen = jnp.where(
            iota((SLIDE_WIDTH, LANES), 0) == wanted(iota((SLIDE_WIDTH, LANES), 1)), 1.0, 0.0
        ).astype(BF16)
        for part in range(3):
            wq_pad[r, :, part * LANES : (part + 1) * LANES] = dot(
                wq_v[:, part * SLIDE_WIDTH : (part + 1) * SLIDE_WIDTH], widen
            ).astype(BF16)
        widen_t = jnp.where(
            iota((LANES, SLIDE_WIDTH), 1) == wanted(iota((LANES, SLIDE_WIDTH), 0)), 1.0, 0.0
        ).astype(BF16)
        wo_pad[r] = dot(widen_t, wo_v[...]).astype(BF16)

    cap = spots.shape[2]

    def place(s):
        hot = jnp.where(iota((TILE_DEV, cap), 0) + first == spots[s], 1.0, 0.0).astype(BF16)
        return dot(hot, arrived[s])

    tokens[...] = place(me)

    def take(s):
        pos_copy(s, s).wait_recv()
        emb_copy(s, s).wait_recv()
        tokens[...] += place(s)

    @pl.loop(1, n // 2)
    def _(i):
        take(flip(me, i, n))

    @pl.loop(0, n // 2)
    def _(i):
        take(flip(me, n - 1 - i, n))

    normed = normalise(tokens[...], slide_gain[...][None, :])

    row_of = iota((TILE_DEV, TILE_DEV), 0)
    regroup = jnp.where(
        iota((TILE_DEV, TILE_DEV), 1) == STRIDE * (row_of % ROWS) + row_of // ROWS, 1.0, 0.0
    ).astype(BF16)
    sorted_rows[...] = dot(regroup, normed).astype(BF16).reshape(TILES, ROWS, SLIDE_WIDTH)
    flat[...] = normed

    def mid_copy(r, g, slot):
        d = g * TILES + r
        return remote(picks.at[r], mids.at[slot], ms.at[d], mr.at[slot], d)

    def bias(rows, step, start):
        lane3 = iota((rows, 3 * LANES), 1)
        valid = iota((rows, 3 * LANES), 0) * step + start + first < total
        value = jnp.where(
            lane3 < LANES, 1.0, jnp.where((lane3 < 2 * LANES) & (~valid), NEGATIVE, 0.0)
        )
        return jnp.where(lane3 % 64 == HEAD_DIM, value, 0.0)

    def project(r):
        return (dot(sorted_rows[r], wq_pad[r]) + bias(ROWS, STRIDE, r)).astype(BF16)

    @pl.loop(0, TILES - 1)
    def _(i):
        r = flip(mine, TILES - 1 - i, TILES)
        picks[r] = project(r)
        for g in range(groups):
            mid_copy(r, g, me).start()

    own_pick = project(mine)
    mids[me] = own_pick
    if groups > 1:
        picks[mine] = own_pick
        for step in range(1, groups):
            mid_copy(mine, (group + step) % groups, me).start()

    lane = iota((TILE_DEV, LANES), 1)
    low = lane < 64

    def half_masks(shape):
        side = iota(shape, 1) < 64
        return side, ~side

    def blend(parts):
        return [jnp.where(low, a, b) for a, b in zip(*parts)]

    def pack(number, divisor, top):
        return jnp.where(
            lane % 64 == 48, divisor, jnp.where(lane % 64 == 49, top, number)
        )

    def local_tile(r):
        made = (dot(flat[...], wq_pad[r]) + bias(TILE_DEV, 1, 0)).astype(BF16)
        q = made[:, :LANES]
        k = made[:, LANES : 2 * LANES]
        v = made[:, 2 * LANES :]
        parts = [soft_parts(q, k, v, mask, None) for mask in half_masks(k.shape)]
        number, divisor, top = blend(parts)
        packed = pack(number, divisor, top)
        row = iota((TILE_DEV, LANES), 0)
        chosen = row % STRIDE == r
        share = number / divisor
        keep = (~chosen) & (row + first < total)
        columns = pl.ds(pl.multiple_of(r * LANES, LANES), LANES)
        attn[:, columns] = jnp.where(keep, share, 0.0).astype(BF16)
        local_pick[r] = jnp.sum(
            jnp.where(chosen, packed, 0.0).reshape(ROWS, STRIDE, LANES), axis=1
        )

    before = 5

    @pl.loop(0, before)
    def _(r):
        local_tile(r)

    def ret_copy(t, slot):
        return remote(ret_out.at[t], ret_in.at[slot], rs.at[t], rr.at[slot], group * TILES + t)

    @pl.loop(1, n)
    def _(i):
        s = flip(me, n - i, n)
        remote(mids.at[s], mids.at[s], ms.at[s], mr.at[s], s).wait_recv()

    far_q = mids[pl.ds(group * TILES, TILES), :, :LANES].reshape(TILES * ROWS, LANES)
    far_k = mids[:, :, LANES : 2 * LANES].reshape(n * ROWS, LANES)
    far_v = mids[:, :, 2 * LANES :].reshape(n * ROWS, LANES)
    far_parts = []
    shape = (TILES * ROWS, n * ROWS)
    for half, mask in enumerate(half_masks(far_k.shape)):
        both = (iota(shape, 0) % 2 == half) & (iota(shape, 1) % 2 == half)
        far_parts.append(soft_parts(far_q, far_k, far_v, mask, jnp.where(both, 2.0, 1.0)))
    ret_out[...] = pack(*blend(far_parts)).reshape(TILES, ROWS, LANES)

    @pl.loop(0, TILES - 1)
    def _(i):
        ret_copy(flip(mine, TILES - 1 - i, TILES), mine).start()

    ret_in[mine] = ret_out[mine]

    @pl.loop(before, TILES)
    def _(r):
        local_tile(r)

    tokens[...] += dot(attn[...], wo_pad[...].reshape(TILES * LANES, SLIDE_WIDTH))

    @pl.loop(0, TILES - 1)
    def _(i):
        t = flip(mine, TILES - 1 - i, TILES)
        ret_copy(t, t).wait_recv()

    joint = []
    small = iota((ROWS, LANES), 1)
    for r in range(TILES):
        here, there = local_pick[r], ret_in[r]

        def joined(at):
            top = jnp.maximum(here[:, at + 1 : at + 2], there[:, at + 1 : at + 2])
            a = jnp.exp2((here[:, at + 1 : at + 2] - top) * C)
            b = jnp.exp2((there[:, at + 1 : at + 2] - top) * C)
            return (a * here + b * there) / (
                a * here[:, at : at + 1] + b * there[:, at : at + 1]
            )

        share = jnp.where(small < 64, joined(48), joined(112))
        share = jnp.where(small % 64 < HEAD_DIM, share, 0.0)
        valid = iota((ROWS, LANES), 0) * STRIDE + r + first < total
        share = jnp.where(valid, share, 0.0).astype(BF16)
        joint.append(dot(share, wo_pad[r])[:, None, :])
    added = jnp.concatenate(joint, axis=1).reshape(TILE_DEV, SLIDE_WIDTH)
    acc = tokens[...] + added
    out[...] = jnp.where(iota((TILE_DEV, 1), 0) + first < total, acc, 0.0).astype(BF16)

    @pl.loop(0, n - 1)
    def _(i):
        d = flip(me, n - 1 - i, n)
        pos_copy(d, me).wait_send()
        emb_copy(d, me).wait_send()
        mid_copy(d % TILES, d // TILES, me).wait_send()

    @pl.loop(0, TILES - 1)
    def _(i):
        ret_copy(flip(mine, TILES - 1 - i, TILES), mine).wait_send()


def shards(n, held_feats, held_pos, tile_count, tile_gain, w_tile, slide_gain, w_qkv, w_out):
    slots, width = held_feats.shape[2:]
    cap = slots // n
    vmem = pl.BlockSpec(memory_space=pltpu.VMEM)
    hbm = pl.BlockSpec(memory_space=pl.ANY)
    smem = pl.BlockSpec(memory_space=pltpu.SMEM)
    dma = pltpu.SemaphoreType.DMA
    result = pl.pallas_call(
        functools.partial(kernel, n),
        out_shape=jax.ShapeDtypeStruct((TILE_DEV, SLIDE_WIDTH), BF16),
        in_specs=[hbm, vmem, smem, vmem, hbm, vmem, hbm, hbm],
        out_specs=vmem,
        scratch_shapes=[
            pltpu.VMEM((n, cap, width), BF16),
            pltpu.VMEM(w_tile.shape, BF16),
            pltpu.VMEM(w_qkv.shape, BF16),
            pltpu.VMEM(w_out.shape, BF16),
            pltpu.VMEM((TILES, SLIDE_WIDTH, 3 * LANES), BF16),
            pltpu.VMEM((TILES, LANES, SLIDE_WIDTH), BF16),
            pltpu.VMEM((n, cap, SLIDE_WIDTH), BF16),
            pltpu.VMEM((n, cap, SLIDE_WIDTH), BF16),
            pltpu.VMEM((n, 1, cap), jnp.int32),
            pltpu.VMEM((TILE_DEV, SLIDE_WIDTH), F32),
            pltpu.VMEM((TILE_DEV, SLIDE_WIDTH), BF16),
            pltpu.VMEM((TILES, ROWS, SLIDE_WIDTH), BF16),
            pltpu.VMEM((TILES, ROWS, 3 * LANES), BF16),
            pltpu.VMEM((n, ROWS, 3 * LANES), BF16),
            pltpu.VMEM((TILES, ROWS, LANES), F32),
            pltpu.VMEM((TILES, ROWS, LANES), F32),
            pltpu.VMEM((TILE_DEV, TILES * LANES), BF16),
            pltpu.VMEM((TILES, ROWS, LANES), F32),
            dma((n,)), dma((3,)),
            dma((n,)), dma((n,)), dma((n,)), dma((n,)),
            dma((n,)), dma((n,)), dma((TILES,)), dma((TILES,)),
        ],
        compiler_params=pltpu.CompilerParams(
            collective_id=0, has_side_effects=True, vmem_limit_bytes=58 * 1024 * 1024
        ),
        name="slide_layer",
    )(
        held_feats.reshape(n, cap, width),
        held_pos.reshape(n, 1, cap),
        tile_count,
        tile_gain,
        w_tile,
        slide_gain,
        w_qkv,
        w_out,
    )
    return result.reshape(1, TILE_DEV, SLIDE_WIDTH)


def solution(mesh):
    n = mesh.shape["seq"]
    return jax.shard_map(
        functools.partial(shards, n),
        mesh=mesh,
        in_specs=(
            P(("groups", "slide"), "seq", None, None),
            P(("groups", "slide"), "seq", None),
            P(("groups", "slide")),
            P(), P(), P(), P(), P(),
        ),
        out_specs=P(("groups", "slide"), "seq", None),
        check_vma=False,
    )
```
